512 devices in a mesh: seq: 64 (over y_hi, z, core), tp: 8 (over x, y_lo).
Axes of the slice: x: 4, y: 4 (y_hi: 2, y_lo: 2; y = y_hi * 2 + y_lo), z: 16, core: 2. Of those that a mesh axis runs over, the one named last changes fastest.
Arguments:
- queries: bfloat16 [65536, 4096], P('seq', 'tp'), may hold values from -600 to 600
- neighbours: bfloat16 [512, 896, 128], P('seq', 'tp'), may hold values from -6 to 6
- key_weight: bfloat16 [896, 4096], P(None, 'tp'), may hold values from -0.1875 to 0.1875
- value_weight: bfloat16 [896, 4096], P(None, 'tp'), may hold values from -0.1875 to 0.1875
- neighbour_ids: int32 [1024, 2], P('seq'), may hold values from 0 to 511, as said below
Outputs:
- attended: bfloat16 [65536, 4096], P('seq', 'tp')
The draws below stay inside these ranges and needn't reach their ends.
Inputs may be any that keep to these rules, and one draw needn't show every extreme that they name: `neighbour_ids`: block b is stored on index b // 8 of seq. Among the 32 neighbours of the spans of one index of seq, at most 1 are stored on any one index of seq, and exactly 1 on some.
All inputs are finite; a program needn't handle non-finite values.
Results may differ from the reference program's by a relative error of at most 0.014.
Values may be sent and summed in bfloat16 or wider, within the bound.
A program may use at most 64 MiB of HBM per device.

```python
import jax
import jax.numpy as jnp
from jax import lax

HEADS = 32
HDIM = 128
DE = 896
SPAN = 64
NLEN = 128
CH_DEV = 16
NB_DEV = 8
SPANS = 1024
TOKENS = 65536
NBLK = 512
N_SEQ = 64


def draw_queries(key, part):
    key = jax.random.fold_in(key, 11)
    base_key = jax.random.fold_in(key, 0)
    shape = (TOKENS, HEADS * HDIM)
    values = jax.random.truncated_normal(base_key, -4.0, 4.0, shape, jnp.float32)
    return values.astype(jnp.bfloat16)


def draw_neighbour_ids(key, part):
    key = jax.random.fold_in(key, 5)
    order_key, block_key = jax.random.split(key)
    seq_keys = jax.random.split(order_key, N_SEQ)
    orders = jax.vmap(lambda single: jax.random.permutation(single, N_SEQ))(seq_keys)
    slot_index = jnp.arange(2 * CH_DEV) % N_SEQ
    sources = orders[:, slot_index]
    within = jax.random.randint(block_key, (N_SEQ, 2 * CH_DEV), 0, NB_DEV)
    chosen_ids = sources * NB_DEV + within
    return chosen_ids.reshape(SPANS, 2).astype(jnp.int32)


def steps_of(rng, extent, pieces, smallest, top_value):
    loudness = 1.0
    for position, blocks in pieces:
        draws = jax.random.uniform(jax.random.fold_in(jax.random.fold_in(rng, 6), position), (blocks,), jnp.float32, smallest / len(pieces), top_value / len(pieces))
        loudness = loudness * jnp.repeat(jnp.exp(draws), extent[position] // blocks).reshape((-1,) + (1,) * (len(extent) - 1 - position))
    return loudness


def scatter_about(own_key, extent, scale, reach, pieces=(), dtype=jnp.bfloat16):
    drawn = scale * jax.random.normal(own_key, extent, jnp.float32)
    if pieces:
        drawn = drawn * steps_of(own_key, extent, pieces, -0.22, 0.18)
    return jnp.clip(drawn, -reach, reach).astype(dtype)


def setup_inputs(seed: int = 0) -> dict:
    streams_of = jax.random.split(jax.random.key(seed), 6)
    return {
        "queries": draw_queries(jax.random.fold_in(streams_of[5], 71), 0),
        "neighbours": scatter_about(streams_of[1], (NBLK, DE, NLEN), 1.0, 6.0, ((0, 64), (1, 8))),
        "key_weight": scatter_about(streams_of[2], (DE, HEADS * HDIM), DE ** -0.5, 0.1875, ((1, 8),)),
        "value_weight": scatter_about(streams_of[3], (DE, HEADS * HDIM), DE ** -0.5, 0.1875, ((1, 8),)),
        "neighbour_ids": draw_neighbour_ids(jax.random.fold_in(streams_of[5], 71), 0),
    }


def reference(queries, neighbours, key_weight, value_weight, neighbour_ids):
    feature_rows = jnp.swapaxes(neighbours, 1, 2).reshape(NBLK * NLEN, DE).astype(jnp.float32)
    edge_rows = SPAN - 1

    def one_head(operands):
        w_key, w_value, q_head = operands
        key_rows = jnp.dot(feature_rows, w_key.astype(jnp.float32), precision=lax.Precision.HIGHEST)
        key_rows = key_rows.astype(jnp.bfloat16).reshape(NBLK, NLEN, HDIM)
        value_rows = jnp.dot(feature_rows, w_value.astype(jnp.float32), precision=lax.Precision.HIGHEST)
        value_rows = value_rows.astype(jnp.bfloat16).reshape(NBLK, NLEN, HDIM)
        windows = jnp.concatenate([q_head[edge_rows:], jnp.zeros((edge_rows, HDIM), jnp.bfloat16)], axis=0)
        windows = windows.reshape(SPANS, SPAN, HDIM)
        chosen_keys = key_rows[neighbour_ids]
        chosen_values = value_rows[neighbour_ids]
        scores = jnp.einsum('cqd,cjkd->cjqk', windows.astype(jnp.float32), chosen_keys.astype(jnp.float32)) * (HDIM ** -0.5)
        highest = jnp.max(scores, axis=-1, keepdims=True)
        exponent = jnp.exp(scores - highest)
        totals = jnp.sum(exponent, axis=-1, keepdims=True)
        weights = (exponent / totals).astype(jnp.bfloat16)
        partials = jnp.einsum('cjqk,cjkd->cjqd', weights.astype(jnp.float32), chosen_values.astype(jnp.float32)).astype(jnp.bfloat16)
        log_totals = (highest + jnp.log(totals))[..., 0]
        largest = jnp.max(log_totals, axis=1, keepdims=True)
        shares = jnp.exp(log_totals - largest)
        shares = shares / jnp.sum(shares, axis=1, keepdims=True)
        blended = jnp.sum(shares[..., None] * partials.astype(jnp.float32), axis=1).astype(jnp.bfloat16)
        blended = blended.reshape(TOKENS, HDIM)
        return jnp.concatenate([jnp.zeros((edge_rows, HDIM), jnp.bfloat16), blended[:TOKENS - edge_rows]], axis=0)

    head_results = lax.map(one_head, (
        jnp.transpose(key_weight.reshape(DE, HEADS, HDIM), (1, 0, 2)),
        jnp.transpose(value_weight.reshape(DE, HEADS, HDIM), (1, 0, 2)),
        jnp.transpose(queries.reshape(TOKENS, HEADS, HDIM), (1, 0, 2))))
    return jnp.transpose(head_results, (1, 0, 2)).reshape(TOKENS, HEADS * HDIM)
```

```python
import jax
import jax.numpy as jnp
from jax import lax
from jax.experimental import pallas as pl
from jax.experimental.pallas import tpu as pltpu
from jax.sharding import PartitionSpec as P

HDIM = 128
SPAN = 64


def passed_along(x, axis, by):
    peers = lax.axis_size(axis)
    pairs = [(i, i + by) for i in range(peers) if 0 <= i + by < peers]
    return lax.ppermute(x, axis, pairs)


def attend_kernel(w_ref, x_ref, q_ref, o_ref):
    features = jnp.concatenate([x_ref[0], x_ref[1]], axis=1)
    rows = jnp.dot(w_ref[...], features, preferred_element_type=jnp.float32).astype(jnp.bfloat16)
    columns = q_ref.shape[1]
    for head in range(columns // HDIM):
        at = head * HDIM
        scores = jnp.dot(
            q_ref[:, at : at + HDIM], rows[at : at + HDIM], preferred_element_type=jnp.float32
        ) * (HDIM**-0.5)
        highest = jnp.max(scores, axis=1, keepdims=True)
        exponent = jnp.exp(scores - highest)
        totals = jnp.sum(exponent, axis=1, keepdims=True)
        blended = lax.dot_general(
            exponent.astype(jnp.bfloat16),
            rows[columns + at : columns + at + HDIM],
            (((1,), (1,)), ((), ())),
            preferred_element_type=jnp.float32,
        )
        o_ref[:, at : at + HDIM] = (blended / totals).astype(jnp.bfloat16)


def shards(queries, neighbours, key_weight, value_weight, neighbour_ids):
    tok_rows, columns = queries.shape
    span_count = neighbour_ids.shape[0]
    edge_rows = SPAN - 1
    incoming = passed_along(queries[:edge_rows], "seq", -1)
    windows = jnp.concatenate([queries[edge_rows:], incoming], axis=0)
    stored = lax.all_gather(neighbours, "seq", axis=0, tiled=True)
    chosen = stored[neighbour_ids.reshape(-1)]
    features = lax.all_gather(chosen, "tp", axis=1, tiled=True)
    weights = jnp.concatenate([key_weight, value_weight], axis=1).T
    depth = weights.shape[1]
    blended = pl.pallas_call(
        attend_kernel,
        out_shape=jax.ShapeDtypeStruct((tok_rows, columns), jnp.bfloat16),
        grid=(span_count,),
        in_specs=[
            pl.BlockSpec((2 * columns, depth), lambda i: (0, 0)),
            pl.BlockSpec((2, depth, features.shape[2]), lambda i: (i, 0, 0)),
            pl.BlockSpec((SPAN, columns), lambda i: (i, 0)),
        ],
        out_specs=pl.BlockSpec((SPAN, columns), lambda i: (i, 0)),
        compiler_params=pltpu.CompilerParams(vmem_limit_bytes=40 * 1024 * 1024),
    )(weights, features, windows)
    carried = passed_along(blended[tok_rows - edge_rows :], "seq", 1)
    return jnp.concatenate([carried, blended[: tok_rows - edge_rows]], axis=0)


def solution(mesh):
    in_specs = (P("seq", "tp"), P("seq", "tp", None), P(None, "tp"), P(None, "tp"), P("seq", None))
    out_specs = P("seq", "tp")
    return jax.shard_map(shards, mesh=mesh, in_specs=in_specs, out_specs=out_specs, check_vma=False)
```

```python
import functools

import jax
import jax.numpy as jnp
from jax import lax
from jax.experimental import pallas as pl
from jax.experimental.pallas import tpu as pltpu
from jax.sharding import PartitionSpec as P

HDIM = 128
SPAN = 64
ZS = 16
XS = 4
CHUNKS = (32, 32, 48)
LAGS = (0, 6, 12)
MESH = pl.DeviceIdType.MESH


def passed_along(x, axis, by):
    peers = lax.axis_size(axis)
    pairs = [(i, i + by) for i in range(peers) if 0 <= i + by < peers]
    return lax.ppermute(x, axis, pairs)


def heads_of_span(weights, features, queries, head_count):
    rows = sum(
        jnp.dot(w, f, preferred_element_type=jnp.float32) for w, f in zip(weights, features)
    ).astype(jnp.bfloat16)
    columns = head_count * HDIM
    results = []
    for head in range(head_count):
        at = head * HDIM
        scores = jnp.dot(
            queries[:, at : at + HDIM], rows[at : at + HDIM], preferred_element_type=jnp.float32
        ) * (HDIM**-0.5)
        highest = jnp.max(scores, axis=1, keepdims=True)
        exponent = jnp.exp(scores - highest)
        totals = jnp.sum(exponent, axis=1, keepdims=True)
        blended = lax.dot_general(
            exponent.astype(jnp.bfloat16),
            rows[columns + at : columns + at + HDIM],
            (((1,), (1,)), ((), ())),
            preferred_element_type=jnp.float32,
        )
        results.append((blended / totals).astype(jnp.bfloat16))
    return jnp.concatenate(results, axis=1)


def ring_events(chunks):
    events = []
    for q in range(chunks):
        for step in range(1, ZS // 2 + 1):
            events.append((LAGS[q] + step, 0, ("ring", q, step)))
        done = LAGS[q] + ZS // 2
        events.append((done, 1, ("pick", q)))
        events.append((done + 3, 2, ("sort", q)))
    return [what for _, _, what in sorted(events)]


def kernel(
    ids_ref, table_ref, stored_ref, weight_ref, window_ref, out_ref, *scratch, n_chunks, head_count
):
    n = n_chunks
    gathered, picked, slots, sorted_, features = (scratch[i * n : (i + 1) * n] for i in range(5))
    (weights, queries, results, tables, table_smem, send_sems, recv_sems, local_sems, back_send, back_recv) = (
        scratch[5 * n :]
    )
    s, t = lax.axis_index("seq"), lax.axis_index("tp")
    h, z, c = s // (2 * ZS), (s // 2) % ZS, s % 2
    x, l = t // 2, t % 2
    columns = head_count * HDIM
    spans = out_ref.shape[0] // SPAN
    mine = spans // XS
    counter = [0, 0]
    sent = []

    def at_seq(h_, z_, c_):
        return (h_ * (2 * ZS) + z_ * 2 + c_, t)

    def at_tp(x_, l_):
        return (s, x_ * 2 + l_)

    def send(src, dst, device):
        i = counter[0]
        counter[0] += 1
        copy = pltpu.make_async_remote_copy(
            src_ref=src,
            dst_ref=dst,
            send_sem=send_sems.at[i],
            recv_sem=recv_sems.at[i],
            device_id=device,
            device_id_type=MESH,
        )
        copy.start()
        sent.append(copy)
        return copy

    def local(src, dst):
        i = counter[1]
        counter[1] += 1
        copy = pltpu.make_async_copy(src, dst, local_sems.at[i])
        copy.start()
        return copy

    right, left = at_seq(h, (z + 1) % ZS, c), at_seq(h, (z + ZS - 1) % ZS, c)
    sides = [(0, 1), (1, 0), (1, 1)]
    side_devices = [at_seq((h + a) % 2, z, (c + b) % 2) for a, b in sides]
    x_of = [(x + d) % XS for d in range(XS)]
    other_core = side_devices[0]

    own_stored = []
    first = 0
    for q in range(n):
        count = CHUNKS[q]
        own_stored.append(local(stored_ref.at[:, pl.ds(first, count), :], gathered[q].at[z]))
        first += count
    own_weight = local(weight_ref, weights.at[x])
    own_table = local(table_ref, table_smem.at[0])

    barrier = pltpu.get_barrier_semaphore()
    partners = [right, left] + side_devices
    partners += [at_tp(x_of[d], (l + e) % 2) for d in range(XS) for e in range(2) if (d, e) != (0, 0)]
    for partner in partners:
        pl.semaphore_signal(barrier, inc=1, device_id=partner, device_id_type=MESH)
    pl.semaphore_wait(barrier, len(partners))

    moved_tables = [
        send(table_ref, tables.at[i], device) for i, device in enumerate(side_devices)
    ]

    half = stored_ref.shape[0] // 2
    moving = {}

    def ring_step(q, step):
        for side in range(2):
            for part in range(2):
                if step == ZS // 2 and side != part:
                    continue
                if step == 1:
                    if side == 0 and part == 0:
                        own_stored[q].wait()
                else:
                    moving[(q, step - 1, side, part)].wait_recv()
                owner = (z + (ZS - step + 1 if side == 0 else step - 1)) % ZS
                block = gathered[q].at[owner, pl.ds(part * half, half)]
                moving[(q, step, side, part)] = send(block, block, right if side == 0 else left)

    def pick(q):
        for side in range(2):
            for part in range(2):
                if side == part:
                    moving[(q, ZS // 2, side, part)].wait_recv()
                else:
                    moving[(q, ZS // 2 - 1, side, part)].wait_recv()
        if q == 0:
            own_table.wait()
            for i, copy in enumerate(moved_tables):
                copy.wait_recv()
            copies = [local(tables.at[i], table_smem.at[i + 1]) for i in range(len(sides))]
            for copy in copies:
                copy.wait()
        for i in range(len(sides) + 1):
            for z_ in range(ZS):
                block = table_smem[i, 0, h * (2 * ZS) + z_ * 2 + c]
                value = gathered[q][z_, block]
                if i == 0:
                    slots[q][h * 2 + c, z_] = value
                else:
                    picked[q][i - 1, z_] = value
        moving[(q, "slots")] = [
            send(picked[q].at[i], slots[q].at[h * 2 + c], device)
            for i, device in enumerate(side_devices)
        ]

    def sort(q):
        for copy in moving[(q, "slots")]:
            copy.wait_recv()
        count = CHUNKS[q]
        for r in range(2 * spans):
            source = ids_ref[r] // 8
            side = (source // (2 * ZS)) * 2 + source % 2
            sorted_[q][r // (2 * mine), r % (2 * mine)] = slots[q][side, (source // 2) % ZS]
        place = pl.ds(pl.multiple_of(t * count, 16), count)
        moving[(q, "sorted")] = [
            send(sorted_[q].at[x_of[d]], features[q].at[:, place, :], at_tp(x_of[d], (l + e) % 2))
            for d in range(XS)
            for e in range(2)
            if (d, e) != (0, 0)
        ]
        moving[(q, "own")] = local(sorted_[q].at[x], features[q].at[:, place, :])

    weight_half = weights.shape[1] // 2
    quarter = weight_half // 2
    own_rows = pl.ds(pl.multiple_of(c * weight_half, 16), weight_half)

    def begin_side_work():
        own_weight.wait()
        part = weights.at[x, own_rows]
        moving["w+"] = send(part, part, at_tp(x_of[1], l))
        moving["w-"] = send(part, part, at_tp(x_of[3], l))
        rows = 2 * mine * SPAN // 2
        for d in range(1, XS):
            start = pl.multiple_of(x_of[d] * rows, 16)
            moving[("q", d)] = send(window_ref.at[pl.ds(start, rows)], queries.at[x], at_tp(x_of[d], l))
        start = pl.multiple_of(x * rows, 16)
        moving[("q", 0)] = local(window_ref.at[pl.ds(start, rows)], queries.at[x])

    def forward_weights():
        for key, to, frm, k in (("w+", 1, 3, 0), ("w-", 3, 1, 1)):
            moving[key].wait_recv()
            rows = pl.ds(pl.multiple_of(c * weight_half + k * quarter, 16), quarter)
            part = weights.at[x_of[frm], rows]
            moving[key + "far"] = send(part, part, at_tp(x_of[to], l))
            part = weights.at[x_of[frm], own_rows]
            moving[key + "core"] = send(part, part, other_core)

    def finish_weights():
        for key in ("w+", "w-"):
            moving[key + "far"].wait_recv()
        part = weights.at[x_of[2], own_rows]
        moving["wfarcore"] = send(part, part, other_core)

    what_ran = 0
    for what in ring_events(n):
        if what[0] == "ring":
            ring_step(what[1], what[2])
        elif what[0] == "pick":
            pick(what[1])
        else:
            sort(what[1])
        what_ran += 1
        if what_ran == 1:
            begin_side_work()
        if what == ("pick", 0):
            forward_weights()
        if what == ("pick", n - 1):
            finish_weights()

    for d in range(XS):
        moving[("q", d)].wait() if d == 0 else moving[("q", d)].wait_recv()
    for key in ("w+core", "w-core", "wfarcore"):
        moving[key].wait_recv()
    for q in range(n):
        moving[(q, "own")].wait()
        for copy in moving[(q, "sorted")]:
            copy.wait_recv()

    def back(u, d):
        rows = pl.ds(pl.multiple_of((x * mine + u) * SPAN, SPAN), SPAN)
        return pltpu.make_async_remote_copy(
            src_ref=results.at[u, d],
            dst_ref=out_ref.at[rows],
            send_sem=back_send.at[u, d - 1],
            recv_sem=back_recv.at[u, d - 1],
            device_id=at_tp(x_of[d], l),
            device_id_type=MESH,
        )

    def span_step(u, carry):
        pair = [
            jnp.concatenate([features[q][2 * u], features[q][2 * u + 1]], axis=1) for q in range(n)
        ]
        for d in (2, 1, 3, 0):
            first = 0
            parts = []
            for q in range(n):
                parts.append(weights[x_of[d], :, first : first + 8 * CHUNKS[q]])
                first += 8 * CHUNKS[q]
            rows = queries[x_of[d], pl.ds(pl.multiple_of(u * SPAN, SPAN), SPAN)]
            value = heads_of_span(parts, pair, rows, head_count)
            if d == 0:
                out_ref[pl.ds(pl.multiple_of((x * mine + u) * SPAN, SPAN), SPAN)] = value
            else:
                results[u, d] = value
                back(u, d).start()
        return carry

    lax.fori_loop(0, mine, span_step, 0)

    for copy in sent:
        copy.wait_send()
    for u in range(mine):
        for d in range(1, XS):
            back(u, d).wait()


def shards(queries, neighbours, key_weight, value_weight, neighbour_ids):
    tok_rows, columns = queries.shape
    span_count = neighbour_ids.shape[0]
    seq_count = lax.axis_size("seq")
    blocks, depth, length = neighbours.shape
    tps = lax.axis_size("tp")
    edge_rows = SPAN - 1
    incoming = passed_along(queries[:edge_rows], "seq", -1)
    windows = jnp.concatenate([queries[edge_rows:], incoming], axis=0)
    weights = jnp.concatenate([key_weight, value_weight], axis=1).T.reshape(2 * columns, tps, depth)
    first, parts = 0, []
    for count in CHUNKS:
        parts.append(weights[:, :, first : first + count].reshape(2 * columns, tps * count))
        first += count
    weights = jnp.concatenate(parts, axis=1)
    ids = neighbour_ids.reshape(-1)
    wanted = (ids // blocks)[None, :] == jnp.arange(seq_count)[:, None]
    table = jnp.sum(jnp.where(wanted, (ids % blocks)[None, :], 0), axis=1)
    table = jnp.zeros((8, 128), jnp.int32).at[0, :seq_count].set(table)
    n = len(CHUNKS)
    bf16 = jnp.bfloat16
    mine = span_count // XS
    scratch = [pltpu.VMEM((ZS, blocks, r, length), bf16) for r in CHUNKS]
    scratch += [pltpu.VMEM((3, ZS, r, length), bf16) for r in CHUNKS]
    scratch += [pltpu.VMEM((4, ZS, r, length), bf16) for r in CHUNKS]
    scratch += [pltpu.VMEM((XS, 2 * mine, r, length), bf16) for r in CHUNKS]
    scratch += [pltpu.VMEM((2 * mine, tps * r, length), bf16) for r in CHUNKS]
    scratch += [
        pltpu.VMEM((XS, 2 * columns, depth * tps), bf16),
        pltpu.VMEM((XS, mine * SPAN, columns), bf16),
        pltpu.VMEM((mine, XS, SPAN, columns), bf16),
        pltpu.VMEM((3, 8, 128), jnp.int32),
        pltpu.SMEM((4, 8, 128), jnp.int32),
        pltpu.SemaphoreType.DMA((160,)),
        pltpu.SemaphoreType.DMA((160,)),
        pltpu.SemaphoreType.DMA((32,)),
        pltpu.SemaphoreType.DMA((mine, XS - 1)),
        pltpu.SemaphoreType.DMA((mine, XS - 1)),
    ]
    blended = pl.pallas_call(
        functools.partial(kernel, n_chunks=n, head_count=columns // HDIM),
        out_shape=jax.ShapeDtypeStruct((tok_rows, columns), bf16),
        in_specs=[
            pl.BlockSpec(memory_space=pltpu.SMEM),
            pl.BlockSpec(memory_space=pltpu.VMEM),
            pl.BlockSpec(memory_space=pl.ANY),
            pl.BlockSpec(memory_space=pl.ANY),
            pl.BlockSpec(memory_space=pltpu.VMEM),
        ],
        out_specs=pl.BlockSpec(memory_space=pltpu.VMEM),
        scratch_shapes=scratch,
        compiler_params=pltpu.CompilerParams(
            collective_id=0, has_side_effects=True, vmem_limit_bytes=50 * 1024 * 1024
        ),
    )(ids, table, neighbours, weights, windows)
    carried = passed_along(blended[tok_rows - edge_rows :], "seq", 1)
    return jnp.concatenate([carried, blended[: tok_rows - edge_rows]], axis=0)


def solution(mesh):
    in_specs = (P("seq", "tp"), P("seq", "tp", None), P(None, "tp"), P(None, "tp"), P("seq", None))
    out_specs = P("seq", "tp")
    return jax.shard_map(shards, mesh=mesh, in_specs=in_specs, out_specs=out_specs, check_vma=False)
```

```python
import functools

import jax
import jax.numpy as jnp
from jax import lax
from jax.experimental import pallas as pl
from jax.experimental.pallas import tpu as pltpu
from jax.sharding import PartitionSpec as P

HDIM = 128
SPAN = 64
ZS = 16
XS = 4
PARTS = 4
MESH = pl.DeviceIdType.MESH


def heads_of_span(rows, queries, head_count):
    columns = head_count * HDIM
    results = []
    for head in range(head_count):
        at = head * HDIM
        scores = jnp.dot(
            queries[:, at : at + HDIM], rows[at : at + HDIM], preferred_element_type=jnp.float32
        ) * (HDIM**-0.5)
        highest = jnp.max(scores, axis=1, keepdims=True)
        exponent = jnp.exp(scores - highest)
        totals = jnp.sum(exponent, axis=1, keepdims=True)
        blended = lax.dot_general(
            exponent.astype(jnp.bfloat16),
            rows[columns + at : columns + at + HDIM],
            (((1,), (1,)), ((), ())),
            preferred_element_type=jnp.float32,
        )
        results.append((blended / totals).astype(jnp.bfloat16))
    return jnp.concatenate(results, axis=1)


def kernel(
    ids_ref, table_ref, stored_ref, key_ref, value_ref, query_ref, out_ref, *scratch, head_count
):
    gathered = scratch[:ZS]
    (picked, slots, sorted_, features, raw_weights, weights, own_queries, queries, results, blended,
     tables, table_smem, send_sems, recv_sems, local_sems, back_send, back_recv) = scratch[ZS:]
    s, t = lax.axis_index("seq"), lax.axis_index("tp")
    seqs = lax.axis_size("seq")
    h, z, c = s // (2 * ZS), (s // 2) % ZS, s % 2
    x, l = t // 2, t % 2
    columns = head_count * HDIM
    tokens = out_ref.shape[0]
    spans = tokens // SPAN
    mine = spans // XS
    counter = [0, 0]
    sent = []

    def at_tp(x_, l_):
        return (s, x_ * 2 + l_)

    def send(src, dst, device):
        i = counter[0]
        counter[0] += 1
        copy = pltpu.make_async_remote_copy(
            src_ref=src,
            dst_ref=dst,
            send_sem=send_sems.at[i],
            recv_sem=recv_sems.at[i],
            device_id=device,
            device_id_type=MESH,
        )
        copy.start()
        sent.append(copy)
        return copy

    def local(src, dst):
        i = counter[1]
        counter[1] += 1
        copy = pltpu.make_async_copy(src, dst, local_sems.at[i])
        copy.start()
        return copy

    right = (h * (2 * ZS) + (z + 1) % ZS * 2 + c, t)
    left = (h * (2 * ZS) + (z + ZS - 1) % ZS * 2 + c, t)
    after, before = ((s + 1) % seqs, t), ((s + seqs - 1) % seqs, t)
    sides = [(0, 1), (1, 0), (1, 1)]
    side_devices = [
        (((h + a) % 2) * (2 * ZS) + z * 2 + (c + b) % 2, x * 2 + (l + a) % 2) for a, b in sides
    ]
    other_core = side_devices[0]
    x_of = [(x + d) % XS for d in range(XS)]

    own_stored = local(stored_ref, gathered[0])
    own_table = local(table_ref, table_smem.at[0])
    own_raw = [local(key_ref, raw_weights.at[0]), local(value_ref, raw_weights.at[1])]
    own_rows_in = local(query_ref, own_queries.at[pl.ds(0, tokens)])

    barrier = pltpu.get_barrier_semaphore()
    partners = [right, left, after, before] + side_devices
    partners += [at_tp(x_of[d], l) for d in range(1, XS)] + [at_tp(x, 1 - l)]
    for partner in partners:
        pl.semaphore_signal(barrier, inc=1, device_id=partner, device_id_type=MESH)
    pl.semaphore_wait(barrier, len(partners))

    size = stored_ref.shape[0] // PARTS
    ring = {}

    def ring_step(step):
        for part in range(PARTS):
            for side in range(2):
                if step > 1:
                    ring[(step - 1, side, part)].wait_recv()
                if step == ZS // 2 and side != part // (PARTS // 2):
                    continue
                sign = 1 if side == 0 else -1
                blocks = pl.ds(part * size, size)
                ring[(step, side, part)] = send(
                    gathered[sign * (step - 1)].at[blocks],
                    gathered[(sign * step) % ZS].at[blocks],
                    right if side == 0 else left,
                )

    def ring_end():
        for part in range(PARTS):
            ring[(ZS // 2, part // (PARTS // 2), part)].wait_recv()

    slot_copies = []

    def pick(k):
        z_ = (z + (ZS - k)) % ZS
        place = h * (2 * ZS) + z_ * 2 + c
        for i in range(len(sides) + 1):
            value = gathered[k % ZS][table_smem[i, 0, place]]
            if i == 0:
                slots[c, z_] = value
            else:
                picked[i - 1, k % ZS] = value
                slot_copies.append(
                    send(
                        picked.at[i - 1, k % ZS],
                        slots.at[2 * sides[i - 1][0] + c, z_],
                        side_devices[i - 1],
                    )
                )

    side_work = {}
    weight_rows = weights.shape[1] // 2
    quarter = weight_rows // 2
    own_half = pl.ds(pl.multiple_of(c * weight_rows, weight_rows), weight_rows)

    def transpose_weights():
        for copy in own_raw:
            copy.wait()
        for k in range(raw_weights.shape[1] // HDIM):
            part = pl.ds(k * HDIM, HDIM)
            weights[x, own_half, part] = raw_weights[c, part].T
        part = weights.at[x, own_half]
        side_work["w+"] = send(part, part, at_tp(x_of[1], l))
        side_work["w-"] = send(part, part, at_tp(x_of[3], l))
        side_work["core"] = [send(part, part, other_core)]

    def forward_weights():
        for key, to, frm, k in (("w+", 1, 3, 0), ("w-", 3, 1, 1)):
            side_work[key].wait_recv()
            rows = pl.ds(pl.multiple_of(c * weight_rows + k * quarter, quarter), quarter)
            part = weights.at[x_of[frm], rows]
            side_work[key + "far"] = send(part, part, at_tp(x_of[to], l))
            part = weights.at[x_of[frm], own_half]
            side_work["core"].append(send(part, part, other_core))

    def finish_weights():
        for key in ("w+far", "w-far"):
            side_work[key].wait_recv()
        part = weights.at[x_of[2], own_half]
        side_work["core"].append(send(part, part, other_core))

    def send_edge():
        own_rows_in.wait()
        side_work["edge"] = send(
            own_queries.at[pl.ds(0, SPAN)], own_queries.at[pl.ds(tokens, SPAN)], before
        )

    window = queries.shape[1]

    def send_queries():
        side_work["edge"].wait_recv()
        side_work["q"] = []
        for d in range(XS):
            start = pl.multiple_of(x_of[d] * (mine * SPAN) + SPAN - 16, 16)
            src, dst = own_queries.at[pl.ds(start, window)], queries.at[x]
            side_work["q"].append(local(src, dst) if d == 0 else send(src, dst, at_tp(x_of[d], l)))

    own_stored.wait()
    moved_tables = [
        send(table_ref, tables.at[i], device) for i, device in enumerate(side_devices)
    ]
    for step in range(1, ZS // 2 + 1):
        ring_step(step)
        if step == 1:
            send_edge()
            transpose_weights()
        elif step == 2:
            own_table.wait()
            for copy in moved_tables:
                copy.wait_recv()
            copies = [local(tables.at[i], table_smem.at[i + 1]) for i in range(len(sides))]
            for copy in copies:
                copy.wait()
            pick(0)
            send_queries()
        if step > 1:
            pick(step - 1)
            pick(1 - step)
        if step == 5:
            forward_weights()
        if step == 8:
            finish_weights()
    ring_end()
    pick(ZS // 2)

    order = [(i + mine - 1) % mine for i in range(mine)]
    to_handlers, across = {}, {}

    def handler_copy(u, d):
        return send(sorted_.at[x_of[d], u], features.at[u, :, t], at_tp(x_of[d], l))

    def across_copy(u, d):
        part = features.at[u, :, x_of[d] * 2 + l]
        return send(part, part, at_tp(x, 1 - l))

    for copy in slot_copies:
        copy.wait_recv()
    for u in order:
        for x_ in range(XS):
            for j in range(2):
                source = ids_ref[(x_ * mine + u) * 2 + j] // 8
                side = ((source // (2 * ZS) + h) % 2) * 2 + source % 2
                sorted_[x_, u, j] = slots[side, (source // 2) % ZS]
        for d in (2, 1, 3):
            to_handlers[(u, d)] = handler_copy(u, d)
        features[u, :, t] = sorted_[x, u]
        across[(u, 0)] = across_copy(u, 0)
    for u in order:
        for d in (3, 1, 2):
            to_handlers[(u, d)].wait_recv()
            across[(u, d)] = across_copy(u, (XS - d) % XS)

    for i in range(XS):
        side_work["q"][i].wait() if i == 0 else side_work["q"][i].wait_recv()
    for copy in side_work["core"]:
        copy.wait_recv()

    def result_rows(span):
        return pl.ds(pl.multiple_of((span + 1) * SPAN, SPAN), SPAN)

    def back(u, d):
        return pltpu.make_async_remote_copy(
            src_ref=results.at[u, d],
            dst_ref=blended.at[result_rows(x * mine + u)],
            send_sem=back_send.at[u, d - 1],
            recv_sem=back_recv.at[u, d - 1],
            device_id=at_tp(x_of[d], l),
            device_id_type=MESH,
        )

    def features_of(u, j):
        source = ids_ref[(x * mine + u) * 2 + j] // 8
        other = (source // (2 * ZS) + h) % 2 == 1
        parts = []
        for k in range(XS):
            low, high = features[u, j, 2 * k], features[u, j, 2 * k + 1]
            parts += [jnp.where(other, high, low), jnp.where(other, low, high)]
        return jnp.concatenate(parts, axis=0)

    for i, u in enumerate(order):
        for d in range(XS):
            across[(u, d)].wait_recv()
        pair = jnp.concatenate([features_of(u, 0), features_of(u, 1)], axis=1)
        for d in (2, 1, 3, 0):
            rows = jnp.dot(weights[x_of[d]], pair, preferred_element_type=jnp.float32)
            wanted = queries[x_of[d], pl.ds(u * SPAN, SPAN + 16)].astype(jnp.float32)
            wanted = wanted[15 : 15 + SPAN].astype(jnp.bfloat16)
            value = heads_of_span(rows.astype(jnp.bfloat16), wanted, head_count)
            if d == 0:
                blended[result_rows(x * mine + u)] = value
            else:
                results[u, d] = value
                back(u, d).start()
        if i == 1:
            for d in range(1, XS):
                back(order[0], d).wait_recv()
            carried = send(blended.at[pl.ds(tokens, SPAN)], blended.at[pl.ds(0, SPAN)], after)

    for u in order[1:]:
        for d in range(1, XS):
            back(u, d).wait_recv()
    carried.wait_recv()
    for i in range(spans):
        rows = blended[pl.ds(i * SPAN, SPAN + 16)].astype(jnp.float32)[1 : 1 + SPAN]
        if i == 0:
            places = lax.broadcasted_iota(jnp.int32, rows.shape, 0)
            rows = jnp.where((s == 0) & (places < SPAN - 1), 0.0, rows)
        out_ref[pl.ds(i * SPAN, SPAN)] = rows.astype(jnp.bfloat16)
    for copy in sent:
        copy.wait_send()
    for u in order:
        for d in range(1, XS):
            back(u, d).wait_send()


def shards(queries, neighbours, key_weight, value_weight, neighbour_ids):
    tok_rows, columns = queries.shape
    span_count = neighbour_ids.shape[0]
    blocks, depth, length = neighbours.shape
    tps = lax.axis_size("tp")
    ids = neighbour_ids.reshape(-1)
    wanted = (ids // blocks)[None, :] == jnp.arange(1024)[:, None]
    table = jnp.sum(jnp.where(wanted, (ids % blocks)[None, :], 0), axis=1).reshape(8, 128)
    bf16 = jnp.bfloat16
    mine = span_count // XS
    scratch = [pltpu.VMEM((blocks, depth, length), bf16) for _ in range(ZS)]
    scratch += [
        pltpu.VMEM((3, ZS, depth, length), bf16),
        pltpu.VMEM((4, ZS, depth, length), bf16),
        pltpu.VMEM((XS, mine, 2, depth, length), bf16),
        pltpu.VMEM((mine, 2, tps, depth, length), bf16),
        pltpu.VMEM((2, depth * tps, columns), bf16),
        pltpu.VMEM((XS, 2 * columns, depth * tps), bf16),
        pltpu.VMEM((tok_rows + SPAN, columns), bf16),
        pltpu.VMEM((XS, mine * SPAN + 16, columns), bf16),
        pltpu.VMEM((mine, XS, SPAN, columns), bf16),
        pltpu.VMEM((tok_rows + SPAN, columns), bf16),
        pltpu.VMEM((3, 8, 128), jnp.int32),
        pltpu.SMEM((4, 8, 128), jnp.int32),
        pltpu.SemaphoreType.DMA((192,)),
        pltpu.SemaphoreType.DMA((192,)),
        pltpu.SemaphoreType.DMA((16,)),
        pltpu.SemaphoreType.DMA((mine, XS - 1)),
        pltpu.SemaphoreType.DMA((mine, XS - 1)),
    ]
    return pl.pallas_call(
        functools.partial(kernel, head_count=columns // HDIM),
        out_shape=jax.ShapeDtypeStruct((tok_rows, columns), bf16),
        in_specs=[
            pl.BlockSpec(memory_space=pltpu.SMEM),
            pl.BlockSpec(memory_space=pltpu.VMEM),
            pl.BlockSpec(memory_space=pl.ANY),
            pl.BlockSpec(memory_space=pl.ANY),
            pl.BlockSpec(memory_space=pl.ANY),
            pl.BlockSpec(memory_space=pl.ANY),
        ],
        out_specs=pl.BlockSpec(memory_space=pltpu.VMEM),
        scratch_shapes=scratch,
        compiler_params=pltpu.CompilerParams(
            collective_id=0, has_side_effects=True, vmem_limit_bytes=50 * 1024 * 1024
        ),
    )(ids, table, neighbours, key_weight, value_weight, queries)


def solution(mesh):
    in_specs = (P("seq", "tp"), P("seq", "tp", None), P(None, "tp"), P(None, "tp"), P("seq", None))
    out_specs = P("seq", "tp")
    return jax.shard_map(shards, mesh=mesh, in_specs=in_specs, out_specs=out_specs, check_vma=False)
```

```python
import functools

import jax
import jax.numpy as jnp
from jax import lax
from jax.experimental import pallas as pl
from jax.experimental.pallas import tpu as pltpu
from jax.sharding import PartitionSpec as P

HDIM = 128
SPAN = 64
ZS = 16
XS = 4
PARTS = 4
GROUPS = ((2, 1), (3, 0))
FIRST = 1
MESH = pl.DeviceIdType.MESH


def heads_of_span(rows, queries, head_count):
    columns = head_count * HDIM
    results = []
    for head in range(head_count):
        at = head * HDIM
        scores = jnp.dot(
            queries[:, at : at + HDIM], rows[at : at + HDIM], preferred_element_type=jnp.float32
        ) * (HDIM**-0.5)
        highest = jnp.max(scores, axis=1, keepdims=True)
        exponent = jnp.exp(scores - highest)
        totals = jnp.sum(exponent, axis=1, keepdims=True)
        blended = lax.dot_general(
            exponent.astype(jnp.bfloat16),
            rows[columns + at : columns + at + HDIM],
            (((1,), (1,)), ((), ())),
            preferred_element_type=jnp.float32,
        )
        results.append((blended / totals).astype(jnp.bfloat16))
    return jnp.concatenate(results, axis=1)


def kernel(
    ids_ref, table_ref, stored_ref, key_ref, value_ref, query_ref, out_ref, *scratch, head_count
):
    gathered = scratch[:ZS]
    (picked, slots, sorted_, features, raw_weights, weights, own_queries, queries, results, blended,
     tables, table_smem, send_sems, recv_sems, local_sems, back_send, back_recv) = scratch[ZS:]
    s, t = lax.axis_index("seq"), lax.axis_index("tp")
    seqs = lax.axis_size("seq")
    h, z, c = s // (2 * ZS), (s // 2) % ZS, s % 2
    x, l = t // 2, t % 2
    columns = head_count * HDIM
    tokens = out_ref.shape[0]
    spans = tokens // SPAN
    mine = spans // XS
    counter = [0, 0]
    sent = []

    def at_tp(x_, l_):
        return (s, x_ * 2 + l_)

    def send(src, dst, device):
        i = counter[0]
        counter[0] += 1
        copy = pltpu.make_async_remote_copy(
            src_ref=src,
            dst_ref=dst,
            send_sem=send_sems.at[i],
            recv_sem=recv_sems.at[i],
            device_id=device,
            device_id_type=MESH,
        )
        copy.start()
        sent.append(copy)
        return copy

    def local(src, dst):
        i = counter[1]
        counter[1] += 1
        copy = pltpu.make_async_copy(src, dst, local_sems.at[i])
        copy.start()
        return copy

    right = (h * (2 * ZS) + (z + 1) % ZS * 2 + c, t)
    left = (h * (2 * ZS) + (z + ZS - 1) % ZS * 2 + c, t)
    after, before = ((s + 1) % seqs, t), ((s + seqs - 1) % seqs, t)
    sides = [(0, 1), (1, 0), (1, 1)]
    side_devices = [
        (((h + a) % 2) * (2 * ZS) + z * 2 + (c + b) % 2, x * 2 + (l + a) % 2) for a, b in sides
    ]
    other_core = side_devices[0]
    x_of = [(x + d) % XS for d in range(XS)]

    own_stored = local(stored_ref, gathered[0])
    own_table = local(table_ref, table_smem.at[0])
    own_raw = [local(key_ref, raw_weights.at[0]), local(value_ref, raw_weights.at[1])]
    own_rows_in = local(query_ref, own_queries.at[pl.ds(0, tokens)])

    barrier = pltpu.get_barrier_semaphore()
    partners = [right, left, after, before] + side_devices
    partners += [at_tp(x_of[d], l) for d in range(1, XS)] + [at_tp(x, 1 - l)]
    for partner in partners:
        pl.semaphore_signal(barrier, inc=1, device_id=partner, device_id_type=MESH)
    pl.semaphore_wait(barrier, len(partners))

    size = stored_ref.shape[0] // PARTS
    ring = {}

    def ring_step(step):
        for part in range(PARTS):
            for side in range(2):
                if step > 1:
                    ring[(step - 1, side, part)].wait_recv()
                if step == ZS // 2 and side != part // (PARTS // 2):
                    continue
                sign = 1 if side == 0 else -1
                blocks = pl.ds(part * size, size)
                ring[(step, side, part)] = send(
                    gathered[sign * (step - 1)].at[blocks],
                    gathered[(sign * step) % ZS].at[blocks],
                    right if side == 0 else left,
                )

    def ring_end():
        for part in range(PARTS):
            ring[(ZS // 2, part // (PARTS // 2), part)].wait_recv()

    slot_copies = []

    def pick(k):
        z_ = (z + (ZS - k)) % ZS
        place = h * (2 * ZS) + z_ * 2 + c
        for i in range(len(sides) + 1):
            value = gathered[k % ZS][table_smem[i, 0, place]]
            if i == 0:
                slots[c, z_] = value
            else:
                picked[i - 1, k % ZS] = value
                slot_copies.append(
                    send(
                        picked.at[i - 1, k % ZS],
                        slots.at[2 * sides[i - 1][0] + c, z_],
                        side_devices[i - 1],
                    )
                )

    side_work = {}
    weight_rows = weights.shape[1] // 2
    quarter = weight_rows // 2
    own_half = pl.ds(pl.multiple_of(c * weight_rows, weight_rows), weight_rows)

    def transpose_weights():
        for copy in own_raw:
            copy.wait()
        for k in range(raw_weights.shape[1] // HDIM):
            part = pl.ds(k * HDIM, HDIM)
            weights[x, own_half, part] = raw_weights[c, part].T
        part = weights.at[x, own_half]
        side_work["w+"] = send(part, part, at_tp(x_of[1], l))
        side_work["w-"] = send(part, part, at_tp(x_of[3], l))
        side_work["core"] = [send(part, part, other_core)]

    def forward_weights():
        for key, to, frm, k in (("w+", 1, 3, 0), ("w-", 3, 1, 1)):
            side_work[key].wait_recv()
            rows = pl.ds(pl.multiple_of(c * weight_rows + k * quarter, quarter), quarter)
            part = weights.at[x_of[frm], rows]
            side_work[key + "far"] = send(part, part, at_tp(x_of[to], l))
            part = weights.at[x_of[frm], own_half]
            side_work["core"].append(send(part, part, other_core))

    def finish_weights():
        for key in ("w+far", "w-far"):
            side_work[key].wait_recv()
        part = weights.at[x_of[2], own_half]
        side_work["core"].append(send(part, part, other_core))

    def send_edge():
        own_rows_in.wait()
        side_work["edge"] = send(
            own_queries.at[pl.ds(0, SPAN)], own_queries.at[pl.ds(tokens, SPAN)], before
        )

    window = queries.shape[1]

    def send_queries():
        side_work["edge"].wait_recv()
        side_work["q"] = []
        for d in range(XS):
            start = pl.multiple_of(x_of[d] * (mine * SPAN) + SPAN - 16, 16)
            src, dst = own_queries.at[pl.ds(start, window)], queries.at[x]
            side_work["q"].append(local(src, dst) if d == 0 else send(src, dst, at_tp(x_of[d], l)))

    own_stored.wait()
    moved_tables = [
        send(table_ref, tables.at[i], device) for i, device in enumerate(side_devices)
    ]
    for step in range(1, ZS // 2 + 1):
        ring_step(step)
        if step == 1:
            send_edge()
            transpose_weights()
        elif step == 2:
            own_table.wait()
            for copy in moved_tables:
                copy.wait_recv()
            copies = [local(tables.at[i], table_smem.at[i + 1]) for i in range(len(sides))]
            for copy in copies:
                copy.wait()
            pick(0)
            send_queries()
        if step > 1:
            pick(step - 1)
            pick(1 - step)
        if step == 5:
            forward_weights()
        if step == 8:
            finish_weights()
    ring_end()
    pick(ZS // 2)

    order = [(i + mine - 1) % mine for i in range(mine)]
    to_handlers, across = {}, {}

    def handler_copy(u, d):
        return send(sorted_.at[x_of[d], u], features.at[u, :, t], at_tp(x_of[d], l))

    def across_copy(u, d):
        part = features.at[u, :, x_of[d] * 2 + l]
        return send(part, part, at_tp(x, 1 - l))

    for copy in slot_copies:
        copy.wait_recv()
    for u in order:
        for x_ in range(XS):
            for j in range(2):
                source = ids_ref[(x_ * mine + u) * 2 + j] // 8
                side = ((source // (2 * ZS) + h) % 2) * 2 + source % 2
                sorted_[x_, u, j] = slots[side, (source // 2) % ZS]
        for d in (2, 1, 3):
            to_handlers[(u, d)] = handler_copy(u, d)
        features[u, :, t] = sorted_[x, u]
        if u in order[:FIRST]:
            across[(u, 0)] = across_copy(u, 0)
    for u in order:
        if u not in order[:FIRST]:
            across[(u, 0)] = across_copy(u, 0)
        for d in (3, 1, 2):
            to_handlers[(u, d)].wait_recv()
            across[(u, d)] = across_copy(u, (XS - d) % XS)

    for i in range(XS):
        side_work["q"][i].wait() if i == 0 else side_work["q"][i].wait_recv()
    for copy in side_work["core"]:
        copy.wait_recv()

    def result_rows(span):
        return pl.ds(pl.multiple_of((span + 1) * SPAN, SPAN), SPAN)

    def back(u, d):
        return pltpu.make_async_remote_copy(
            src_ref=results.at[u, d],
            dst_ref=blended.at[result_rows(x * mine + u)],
            send_sem=back_send.at[u, d - 1],
            recv_sem=back_recv.at[u, d - 1],
            device_id=at_tp(x_of[d], l),
            device_id_type=MESH,
        )

    def features_of(u, j):
        source = ids_ref[(x * mine + u) * 2 + j] // 8
        other = (source // (2 * ZS) + h) % 2 == 1
        parts = []
        for k in range(XS):
            low, high = features[u, j, 2 * k], features[u, j, 2 * k + 1]
            parts += [jnp.where(other, high, low), jnp.where(other, low, high)]
        return jnp.concatenate(parts, axis=0)

    for i, u in enumerate(order):
        for d in range(XS):
            across[(u, d)].wait_recv()
        pair = jnp.concatenate([features_of(u, 0), features_of(u, 1)], axis=1)
        for group in GROUPS:
            projected = {
                d: jnp.dot(weights[x_of[d]], pair, preferred_element_type=jnp.float32).astype(
                    jnp.bfloat16
                )
                for d in group
            }
            for d in group:
                wanted = queries[x_of[d], pl.ds(u * SPAN, SPAN + 16)].astype(jnp.float32)
                wanted = wanted[15 : 15 + SPAN].astype(jnp.bfloat16)
                value = heads_of_span(projected[d], wanted, head_count)
                if d == 0:
                    blended[result_rows(x * mine + u)] = value
                else:
                    results[u, d] = value
            for d in group:
                if d > 0:
                    back(u, d).start()
        if i == 1:
            for d in range(1, XS):
                back(order[0], d).wait_recv()
            carried = send(blended.at[pl.ds(tokens, SPAN)], blended.at[pl.ds(0, SPAN)], after)

    for u in order[1:]:
        for d in range(1, XS):
            back(u, d).wait_recv()
    carried.wait_recv()
    for i in range(spans):
        rows = blended[pl.ds(i * SPAN, SPAN + 16)].astype(jnp.float32)[1 : 1 + SPAN]
        if i == 0:
            places = lax.broadcasted_iota(jnp.int32, rows.shape, 0)
            rows = jnp.where((s == 0) & (places < SPAN - 1), 0.0, rows)
        out_ref[pl.ds(i * SPAN, SPAN)] = rows.astype(jnp.bfloat16)
    for copy in sent:
        copy.wait_send()
    for u in order:
        for d in range(1, XS):
            back(u, d).wait_send()


def shards(queries, neighbours, key_weight, value_weight, neighbour_ids):
    tok_rows, columns = queries.shape
    span_count = neighbour_ids.shape[0]
    blocks, depth, length = neighbours.shape
    tps = lax.axis_size("tp")
    ids = neighbour_ids.reshape(-1)
    wanted = (ids // blocks)[None, :] == jnp.arange(1024)[:, None]
    table = jnp.sum(jnp.where(wanted, (ids % blocks)[None, :], 0), axis=1).reshape(8, 128)
    bf16 = jnp.bfloat16
    mine = span_count // XS
    scratch = [pltpu.VMEM((blocks, depth, length), bf16) for _ in range(ZS)]
    scratch += [
        pltpu.VMEM((3, ZS, depth, length), bf16),
        pltpu.VMEM((4, ZS, depth, length), bf16),
        pltpu.VMEM((XS, mine, 2, depth, length), bf16),
        pltpu.VMEM((mine, 2, tps, depth, length), bf16),
        pltpu.VMEM((2, depth * tps, columns), bf16),
        pltpu.VMEM((XS, 2 * columns, depth * tps), bf16),
        pltpu.VMEM((tok_rows + SPAN, columns), bf16),
        pltpu.VMEM((XS, mine * SPAN + 16, columns), bf16),
        pltpu.VMEM((mine, XS, SPAN, columns), bf16),
        pltpu.VMEM((tok_rows + SPAN, columns), bf16),
        pltpu.VMEM((3, 8, 128), jnp.int32),
        pltpu.SMEM((4, 8, 128), jnp.int32),
        pltpu.SemaphoreType.DMA((192,)),
        pltpu.SemaphoreType.DMA((192,)),
        pltpu.SemaphoreType.DMA((16,)),
        pltpu.SemaphoreType.DMA((mine, XS - 1)),
        pltpu.SemaphoreType.DMA((mine, XS - 1)),
    ]
    return pl.pallas_call(
        functools.partial(kernel, head_count=columns // HDIM),
        out_shape=jax.ShapeDtypeStruct((tok_rows, columns), bf16),
        in_specs=[
            pl.BlockSpec(memory_space=pltpu.SMEM),
            pl.BlockSpec(memory_space=pltpu.VMEM),
            pl.BlockSpec(memory_space=pl.ANY),
            pl.BlockSpec(memory_space=pl.ANY),
            pl.BlockSpec(memory_space=pl.ANY),
            pl.BlockSpec(memory_space=pl.ANY),
        ],
        out_specs=pl.BlockSpec(memory_space=pltpu.VMEM),
        scratch_shapes=scratch,
        compiler_params=pltpu.CompilerParams(
            collective_id=0, has_side_effects=True, vmem_limit_bytes=63 * 1024 * 1024
        ),
    )(ids, table, neighbours, key_weight, value_weight, queries)


def solution(mesh):
    in_specs = (P("seq", "tp"), P("seq", "tp", None), P(None, "tp"), P(None, "tp"), P("seq", None))
    out_specs = P("seq", "tp")
    return jax.shard_map(shards, mesh=mesh, in_specs=in_specs, out_specs=out_specs, check_vma=False)
```

```python
import functools

import jax
import jax.numpy as jnp
from jax import lax
from jax.experimental import pallas as pl
from jax.experimental.pallas import tpu as pltpu
from jax.sharding import PartitionSpec as P

HDIM = 128
SPAN = 64
ZS = 16
XS = 4
PARTS = 4
GROUPS = ((2, 1), (3, 0))
FIRST = 1
AHEAD = 3
LATE = True
EARLY_OUT = True
WEIGHTS_AT = (4, 6)
QUERIES_AT = 6
MESH = pl.DeviceIdType.MESH


def heads_of_span(rows, queries, head_count):
    columns = head_count * HDIM
    results = []
    for head in range(head_count):
        at = head * HDIM
        scores = jnp.dot(
            queries[:, at : at + HDIM], rows[at : at + HDIM], preferred_element_type=jnp.float32
        ) * (HDIM**-0.5)
        highest = jnp.max(scores, axis=1, keepdims=True)
        exponent = jnp.exp(scores - highest)
        totals = jnp.sum(exponent, axis=1, keepdims=True)
        blended = lax.dot_general(
            exponent.astype(jnp.bfloat16),
            rows[columns + at : columns + at + HDIM],
            (((1,), (1,)), ((), ())),
            preferred_element_type=jnp.float32,
        )
        results.append((blended / totals).astype(jnp.bfloat16))
    return jnp.concatenate(results, axis=1)


def kernel(
    ids_ref, table_ref, stored_ref, key_ref, value_ref, query_ref, out_ref, *scratch, head_count
):
    gathered = scratch[:ZS]
    (picked, slots, sorted_, features, raw_weights, weights, own_queries, queries, results, blended,
     tables, table_smem, send_sems, recv_sems, local_sems, back_send, back_recv) = scratch[ZS:]
    s, t = lax.axis_index("seq"), lax.axis_index("tp")
    seqs = lax.axis_size("seq")
    h, z, c = s // (2 * ZS), (s // 2) % ZS, s % 2
    x, l = t // 2, t % 2
    columns = head_count * HDIM
    tokens = out_ref.shape[0]
    spans = tokens // SPAN
    mine = spans // XS
    counter = [0, 0]
    sent = []

    def at_tp(x_, l_):
        return (s, x_ * 2 + l_)

    def send(src, dst, device):
        i = counter[0]
        counter[0] += 1
        copy = pltpu.make_async_remote_copy(
            src_ref=src,
            dst_ref=dst,
            send_sem=send_sems.at[i],
            recv_sem=recv_sems.at[i],
            device_id=device,
            device_id_type=MESH,
        )
        copy.start()
        sent.append(copy)
        return copy

    def local(src, dst):
        i = counter[1]
        counter[1] += 1
        copy = pltpu.make_async_copy(src, dst, local_sems.at[i])
        copy.start()
        return copy

    right = (h * (2 * ZS) + (z + 1) % ZS * 2 + c, t)
    left = (h * (2 * ZS) + (z + ZS - 1) % ZS * 2 + c, t)
    after, before = ((s + 1) % seqs, t), ((s + seqs - 1) % seqs, t)
    sides = [(0, 1), (1, 0), (1, 1)]
    side_devices = [
        (((h + a) % 2) * (2 * ZS) + z * 2 + (c + b) % 2, x * 2 + (l + a) % 2) for a, b in sides
    ]
    other_core = side_devices[0]
    x_of = [(x + d) % XS for d in range(XS)]

    own_stored = local(stored_ref, gathered[0])
    own_table = local(table_ref, table_smem.at[0])
    own_raw = [local(key_ref, raw_weights.at[0]), local(value_ref, raw_weights.at[1])]
    own_rows_in = local(query_ref, own_queries.at[pl.ds(0, tokens)])

    barrier = pltpu.get_barrier_semaphore()
    partners = [right, left, after, before] + side_devices
    partners += [at_tp(x_of[d], l) for d in range(1, XS)] + [at_tp(x, 1 - l)]
    for partner in partners:
        pl.semaphore_signal(barrier, inc=1, device_id=partner, device_id_type=MESH)
    pl.semaphore_wait(barrier, len(partners))

    size = stored_ref.shape[0] // PARTS
    ring = {}

    def ring_step(step):
        for part in range(PARTS):
            for side in range(2):
                if step > 1:
                    ring[(step - 1, side, part)].wait_recv()
                if step == ZS // 2 and side != part // (PARTS // 2):
                    continue
                sign = 1 if side == 0 else -1
                blocks = pl.ds(part * size, size)
                ring[(step, side, part)] = send(
                    gathered[sign * (step - 1)].at[blocks],
                    gathered[(sign * step) % ZS].at[blocks],
                    right if side == 0 else left,
                )
            if LATE:
                pick_waiting()
        if step == 2:
            waiting.append(0)
        if step > 1:
            waiting.extend([step - 1, 1 - step])
        while waiting and not LATE:
            pick_waiting()

    def ring_end():
        while waiting:
            pick_waiting()
        for part in range(PARTS):
            ring[(ZS // 2, part // (PARTS // 2), part)].wait_recv()

    slot_copies = []
    waiting = []

    def pick_waiting():
        if waiting:
            pick(waiting.pop(0))

    def pick(k):
        z_ = (z + (ZS - k)) % ZS
        place = h * (2 * ZS) + z_ * 2 + c
        for i in range(len(sides) + 1):
            value = gathered[k % ZS][table_smem[i, 0, place]]
            if i == 0:
                slots[c, z_] = value
            else:
                picked[i - 1, k % ZS] = value
                slot_copies.append(
                    send(
                        picked.at[i - 1, k % ZS],
                        slots.at[2 * sides[i - 1][0] + c, z_],
                        side_devices[i - 1],
                    )
                )

    side_work = {}
    weight_rows = weights.shape[1] // 2
    quarter = weight_rows // 2
    own_half = pl.ds(pl.multiple_of(c * weight_rows, weight_rows), weight_rows)

    def transpose_weights():
        for copy in own_raw:
            copy.wait()
        for k in range(raw_weights.shape[1] // HDIM):
            part = pl.ds(k * HDIM, HDIM)
            weights[x, own_half, part] = raw_weights[c, part].T
        part = weights.at[x, own_half]
        side_work["w+"] = send(part, part, at_tp(x_of[1], l))
        side_work["w-"] = send(part, part, at_tp(x_of[3], l))
        side_work["core"] = [send(part, part, other_core)]

    def forward_weights():
        for key, to, frm, k in (("w+", 1, 3, 0), ("w-", 3, 1, 1)):
            side_work[key].wait_recv()
            rows = pl.ds(pl.multiple_of(c * weight_rows + k * quarter, quarter), quarter)
            part = weights.at[x_of[frm], rows]
            side_work[key + "far"] = send(part, part, at_tp(x_of[to], l))
            part = weights.at[x_of[frm], own_half]
            side_work["core"].append(send(part, part, other_core))

    def finish_weights():
        for key in ("w+far", "w-far"):
            side_work[key].wait_recv()
        part = weights.at[x_of[2], own_half]
        side_work["core"].append(send(part, part, other_core))

    def send_edge():
        own_rows_in.wait()
        side_work["edge"] = send(
            own_queries.at[pl.ds(0, SPAN)], own_queries.at[pl.ds(tokens, SPAN)], before
        )

    window = queries.shape[1]

    def send_queries():
        side_work["edge"].wait_recv()
        side_work["q"] = []
        for d in range(XS):
            start = pl.multiple_of(x_of[d] * (mine * SPAN) + SPAN - 16, 16)
            src, dst = own_queries.at[pl.ds(start, window)], queries.at[x]
            side_work["q"].append(local(src, dst) if d == 0 else send(src, dst, at_tp(x_of[d], l)))

    own_stored.wait()
    moved_tables = [
        send(table_ref, tables.at[i], device) for i, device in enumerate(side_devices)
    ]
    for step in range(1, ZS // 2 + 1):
        if step == 2:
            own_table.wait()
            for copy in moved_tables:
                copy.wait_recv()
            copies = [local(tables.at[i], table_smem.at[i + 1]) for i in range(len(sides))]
            for copy in copies:
                copy.wait()
        ring_step(step)
        if step == 1:
            send_edge()
            transpose_weights()
        if step == WEIGHTS_AT[0]:
            forward_weights()
        if step == WEIGHTS_AT[1]:
            finish_weights()
        if step == QUERIES_AT:
            send_queries()
    ring_end()
    pick(ZS // 2)

    order = [(i + mine - 1) % mine for i in range(mine)]
    to_handlers, across = {}, {}

    def handler_copy(u, d):
        return send(sorted_.at[x_of[d], u], features.at[u, :, t], at_tp(x_of[d], l))

    def across_copy(u, d):
        part = features.at[u, :, x_of[d] * 2 + l]
        return send(part, part, at_tp(x, 1 - l))

    for copy in slot_copies:
        copy.wait_recv()
    for u in order:
        for x_ in range(XS):
            for j in range(2):
                source = ids_ref[(x_ * mine + u) * 2 + j] // 8
                side = ((source // (2 * ZS) + h) % 2) * 2 + source % 2
                sorted_[x_, u, j] = slots[side, (source // 2) % ZS]
        for d in (2, 1, 3):
            to_handlers[(u, d)] = handler_copy(u, d)
        features[u, :, t] = sorted_[x, u]
        if u in order[:FIRST]:
            across[(u, 0)] = across_copy(u, 0)

    def forward(u):
        if u not in order[:FIRST]:
            across[(u, 0)] = across_copy(u, 0)
        for d in (3, 1, 2):
            to_handlers[(u, d)].wait_recv()
            across[(u, d)] = across_copy(u, (XS - d) % XS)

    for u in order[:AHEAD]:
        forward(u)

    for i in range(XS):
        side_work["q"][i].wait() if i == 0 else side_work["q"][i].wait_recv()
    for copy in side_work["core"]:
        copy.wait_recv()

    def result_rows(span):
        return pl.ds(pl.multiple_of((span + 1) * SPAN, SPAN), SPAN)

    def back(u, d):
        return pltpu.make_async_remote_copy(
            src_ref=results.at[u, d],
            dst_ref=blended.at[result_rows(x * mine + u)],
            send_sem=back_send.at[u, d - 1],
            recv_sem=back_recv.at[u, d - 1],
            device_id=at_tp(x_of[d], l),
            device_id_type=MESH,
        )

    def features_of(u, j):
        source = ids_ref[(x * mine + u) * 2 + j] // 8
        other = (source // (2 * ZS) + h) % 2 == 1
        parts = []
        for k in range(XS):
            low, high = features[u, j, 2 * k], features[u, j, 2 * k + 1]
            parts += [jnp.where(other, high, low), jnp.where(other, low, high)]
        return jnp.concatenate(parts, axis=0)

    for i, u in enumerate(order):
        for d in range(XS):
            across[(u, d)].wait_recv()
        pair = jnp.concatenate([features_of(u, 0), features_of(u, 1)], axis=1)
        for group in GROUPS:
            projected = {
                d: jnp.dot(weights[x_of[d]], pair, preferred_element_type=jnp.float32).astype(
                    jnp.bfloat16
                )
                for d in group
            }
            for d in group:
                wanted = queries[x_of[d], pl.ds(u * SPAN, SPAN + 16)].astype(jnp.float32)
                wanted = wanted[15 : 15 + SPAN].astype(jnp.bfloat16)
                value = heads_of_span(projected[d], wanted, head_count)
                if d == 0:
                    blended[result_rows(x * mine + u)] = value
                else:
                    results[u, d] = value
            for d in group:
                if d > 0:
                    back(u, d).start()
        if i + AHEAD < mine:
            forward(order[i + AHEAD])
        if i == 1:
            for d in range(1, XS):
                back(order[0], d).wait_recv()
            carried = send(blended.at[pl.ds(tokens, SPAN)], blended.at[pl.ds(0, SPAN)], after)

    def shift_out(i):
        rows = blended[pl.ds(i * SPAN, SPAN + 16)].astype(jnp.float32)[1 : 1 + SPAN]
        if i == 0:
            places = lax.broadcasted_iota(jnp.int32, rows.shape, 0)
            rows = jnp.where((s == 0) & (places < SPAN - 1), 0.0, rows)
        out_ref[pl.ds(i * SPAN, SPAN)] = rows.astype(jnp.bfloat16)

    last = [i for i in range(spans) if not EARLY_OUT or order[-1] in (i % mine, (i - 1) % mine)]
    for u in order[1:]:
        if u == order[-1]:
            carried.wait_recv()
            for i in range(spans):
                if i not in last:
                    shift_out(i)
        for d in range(1, XS):
            back(u, d).wait_recv()
    for i in last:
        shift_out(i)
    for copy in sent:
        copy.wait_send()
    for u in order:
        for d in range(1, XS):
            back(u, d).wait_send()


def shards(queries, neighbours, key_weight, value_weight, neighbour_ids):
    tok_rows, columns = queries.shape
    span_count = neighbour_ids.shape[0]
    blocks, depth, length = neighbours.shape
    tps = lax.axis_size("tp")
    ids = neighbour_ids.reshape(-1)
    wanted = (ids // blocks)[None, :] == jnp.arange(1024)[:, None]
    table = jnp.sum(jnp.where(wanted, (ids % blocks)[None, :], 0), axis=1).reshape(8, 128)
    bf16 = jnp.bfloat16
    mine = span_count // XS
    scratch = [pltpu.VMEM((blocks, depth, length), bf16) for _ in range(ZS)]
    scratch += [
        pltpu.VMEM((3, ZS, depth, length), bf16),
        pltpu.VMEM((4, ZS, depth, length), bf16),
        pltpu.VMEM((XS, mine, 2, depth, length), bf16),
        pltpu.VMEM((mine, 2, tps, depth, length), bf16),
        pltpu.VMEM((2, depth * tps, columns), bf16),
        pltpu.VMEM((XS, 2 * columns, depth * tps), bf16),
        pltpu.VMEM((tok_rows + SPAN, columns), bf16),
        pltpu.VMEM((XS, mine * SPAN + 16, columns), bf16),
        pltpu.VMEM((mine, XS, SPAN, columns), bf16),
        pltpu.VMEM((tok_rows + SPAN, columns), bf16),
        pltpu.VMEM((3, 8, 128), jnp.int32),
        pltpu.SMEM((4, 8, 128), jnp.int32),
        pltpu.SemaphoreType.DMA((192,)),
        pltpu.SemaphoreType.DMA((192,)),
        pltpu.SemaphoreType.DMA((16,)),
        pltpu.SemaphoreType.DMA((mine, XS - 1)),
        pltpu.SemaphoreType.DMA((mine, XS - 1)),
    ]
    return pl.pallas_call(
        functools.partial(kernel, head_count=columns // HDIM),
        out_shape=jax.ShapeDtypeStruct((tok_rows, columns), bf16),
        in_specs=[
            pl.BlockSpec(memory_space=pltpu.SMEM),
            pl.BlockSpec(memory_space=pltpu.VMEM),
            pl.BlockSpec(memory_space=pltpu.HBM),
            pl.BlockSpec(memory_space=pltpu.HBM),
            pl.BlockSpec(memory_space=pltpu.HBM),
            pl.BlockSpec(memory_space=pltpu.HBM),
        ],
        out_specs=pl.BlockSpec(memory_space=pltpu.VMEM),
        scratch_shapes=scratch,
        compiler_params=pltpu.CompilerParams(
            collective_id=0, has_side_effects=True, vmem_limit_bytes=63 * 1024 * 1024
        ),
    )(ids, table, neighbours, key_weight, value_weight, queries)


def solution(mesh):
    in_specs = (P("seq", "tp"), P("seq", "tp", None), P(None, "tp"), P(None, "tp"), P("seq", None))
    out_specs = P("seq", "tp")
    return jax.shard_map(shards, mesh=mesh, in_specs=in_specs, out_specs=out_specs, check_vma=False)
```

```python
import functools

import jax
import jax.numpy as jnp
from jax import lax
from jax.experimental import pallas as pl
from jax.experimental.pallas import tpu as pltpu
from jax.sharding import PartitionSpec as P

HDIM = 128
SPAN = 64
ZS = 16
XS = 4
PARTS = 4
GROUPS = ((2, 1), (3, 0))
FIRST = 1
AHEAD = 3
LATE = True
EARLY_OUT = True
WEIGHTS_AT = (4, 6)
QUERIES_AT = 8
MESH = pl.DeviceIdType.MESH


def heads_of_span(rows, queries, head_count):
    columns = head_count * HDIM
    results = []
    for head in range(head_count):
        at = head * HDIM
        scores = jnp.dot(
            queries[:, at : at + HDIM], rows[at : at + HDIM], preferred_element_type=jnp.float32
        ) * (HDIM**-0.5)
        highest = jnp.max(scores, axis=1, keepdims=True)
        exponent = jnp.exp(scores - highest)
        totals = jnp.sum(exponent, axis=1, keepdims=True)
        blended = lax.dot_general(
            exponent.astype(jnp.bfloat16),
            rows[columns + at : columns + at + HDIM],
            (((1,), (1,)), ((), ())),
            preferred_element_type=jnp.float32,
        )
        results.append((blended / totals).astype(jnp.bfloat16))
    return jnp.concatenate(results, axis=1)


def kernel(
    ids_ref, table_ref, stored_ref, key_ref, value_ref, query_ref, out_ref, *scratch, head_count
):
    gathered = scratch[:ZS]
    (picked, slots, sorted_, features, raw_weights, weights, own_queries, queries, results, blended,
     tables, table_smem, send_sems, recv_sems, local_sems, back_send, back_recv) = scratch[ZS:]
    s, t = lax.axis_index("seq"), lax.axis_index("tp")
    seqs = lax.axis_size("seq")
    h, z, c = s // (2 * ZS), (s // 2) % ZS, s % 2
    x, l = t // 2, t % 2
    columns = head_count * HDIM
    tokens = out_ref.shape[0]
    spans = tokens // SPAN
    mine = spans // XS
    counter = [0, 0]
    sent = []

    def at_tp(x_, l_):
        return (s, x_ * 2 + l_)

    def send(src, dst, device):
        i = counter[0]
        counter[0] += 1
        copy = pltpu.make_async_remote_copy(
            src_ref=src,
            dst_ref=dst,
            send_sem=send_sems.at[i],
            recv_sem=recv_sems.at[i],
            device_id=device,
            device_id_type=MESH,
        )
        copy.start()
        sent.append(copy)
        return copy

    def local(src, dst):
        i = counter[1]
        counter[1] += 1
        copy = pltpu.make_async_copy(src, dst, local_sems.at[i])
        copy.start()
        return copy

    right = (h * (2 * ZS) + (z + 1) % ZS * 2 + c, t)
    left = (h * (2 * ZS) + (z + ZS - 1) % ZS * 2 + c, t)
    after, before = ((s + 1) % seqs, t), ((s + seqs - 1) % seqs, t)
    sides = [(0, 1), (1, 0), (1, 1)]
    side_devices = [
        (((h + a) % 2) * (2 * ZS) + z * 2 + (c + b) % 2, x * 2 + (l + a) % 2) for a, b in sides
    ]
    other_core = side_devices[0]
    x_of = [(x + d) % XS for d in range(XS)]

    own_stored = local(stored_ref, gathered[0])
    own_table = local(table_ref, table_smem.at[0])
    own_raw = [local(key_ref, raw_weights.at[0]), local(value_ref, raw_weights.at[1])]
    own_rows_in = local(query_ref, own_queries.at[pl.ds(0, tokens)])

    barrier = pltpu.get_barrier_semaphore()
    partners = [right, left, after, before] + side_devices
    partners += [at_tp(x_of[d], l) for d in range(1, XS)] + [at_tp(x, 1 - l)]
    for partner in partners:
        pl.semaphore_signal(barrier, inc=1, device_id=partner, device_id_type=MESH)
    pl.semaphore_wait(barrier, len(partners))

    size = stored_ref.shape[0] // PARTS
    ring = {}

    def ring_step(step):
        for part in range(PARTS):
            for side in range(2):
                if step > 1:
                    ring[(step - 1, side, part)].wait_recv()
                if step == ZS // 2 and side != part // (PARTS // 2):
                    continue
                sign = 1 if side == 0 else -1
                blocks = pl.ds(part * size, size)
                ring[(step, side, part)] = send(
                    gathered[sign * (step - 1)].at[blocks],
                    gathered[(sign * step) % ZS].at[blocks],
                    right if side == 0 else left,
                )
            if LATE:
                pick_waiting()
        if step == 2:
            waiting.append(0)
        if step > 1:
            waiting.extend([step - 1, 1 - step])
        while waiting and not LATE:
            pick_waiting()

    def ring_end():
        while waiting:
            pick_waiting()
        for part in range(PARTS):
            ring[(ZS // 2, part // (PARTS // 2), part)].wait_recv()

    slot_copies = []
    waiting = []

    def pick_waiting():
        if waiting:
            pick(waiting.pop(0))

    def pick(k):
        z_ = (z + (ZS - k)) % ZS
        place = h * (2 * ZS) + z_ * 2 + c
        for i in range(len(sides) + 1):
            value = gathered[k % ZS][table_smem[i, 0, place]]
            if i == 0:
                slots[c, z_] = value
            else:
                picked[i - 1, k % ZS] = value
                slot_copies.append(
                    send(
                        picked.at[i - 1, k % ZS],
                        slots.at[2 * sides[i - 1][0] + c, z_],
                        side_devices[i - 1],
                    )
                )

    side_work = {}
    weight_rows = weights.shape[1] // 2
    quarter = weight_rows // 2
    own_half = pl.ds(pl.multiple_of(c * weight_rows, weight_rows), weight_rows)

    def transpose_weights():
        for copy in own_raw:
            copy.wait()
        for k in range(raw_weights.shape[1] // HDIM):
            part = pl.ds(k * HDIM, HDIM)
            weights[x, own_half, part] = raw_weights[c, part].T
        part = weights.at[x, own_half]
        side_work["w+"] = send(part, part, at_tp(x_of[1], l))
        side_work["w-"] = send(part, part, at_tp(x_of[3], l))
        side_work["core"] = [send(part, part, other_core)]

    def forward_weights():
        for key, to, frm, k in (("w+", 1, 3, 0), ("w-", 3, 1, 1)):
            side_work[key].wait_recv()
            rows = pl.ds(pl.multiple_of(c * weight_rows + k * quarter, quarter), quarter)
            part = weights.at[x_of[frm], rows]
            side_work[key + "far"] = send(part, part, at_tp(x_of[to], l))
            part = weights.at[x_of[frm], own_half]
            side_work["core"].append(send(part, part, other_core))

    def finish_weights():
        for key in ("w+far", "w-far"):
            side_work[key].wait_recv()
        part = weights.at[x_of[2], own_half]
        side_work["core"].append(send(part, part, other_core))

    def send_edge():
        own_rows_in.wait()
        side_work["edge"] = send(
            own_queries.at[pl.ds(0, SPAN)], own_queries.at[pl.ds(tokens, SPAN)], before
        )

    window = queries.shape[1]

    def send_queries():
        side_work["edge"].wait_recv()
        side_work["q"] = []
        for d in range(XS):
            start = pl.multiple_of(x_of[d] * (mine * SPAN) + SPAN - 16, 16)
            src, dst = own_queries.at[pl.ds(start, window)], queries.at[x]
            side_work["q"].append(local(src, dst) if d == 0 else send(src, dst, at_tp(x_of[d], l)))

    own_stored.wait()
    moved_tables = [
        send(table_ref, tables.at[i], device) for i, device in enumerate(side_devices)
    ]
    for step in range(1, ZS // 2 + 1):
        if step == 2:
            own_table.wait()
            for copy in moved_tables:
                copy.wait_recv()
            copies = [local(tables.at[i], table_smem.at[i + 1]) for i in range(len(sides))]
            for copy in copies:
                copy.wait()
        ring_step(step)
        if step == 1:
            send_edge()
            transpose_weights()
        if step == WEIGHTS_AT[0]:
            forward_weights()
        if step == WEIGHTS_AT[1]:
            finish_weights()
        if step == QUERIES_AT:
            send_queries()
    ring_end()
    pick(ZS // 2)

    order = [(i + mine - 1) % mine for i in range(mine)]
    to_handlers, across = {}, {}

    def handler_copy(u, d):
        return send(sorted_.at[x_of[d], u], features.at[u, :, t], at_tp(x_of[d], l))

    def across_copy(u, d):
        part = features.at[u, :, x_of[d] * 2 + l]
        return send(part, part, at_tp(x, 1 - l))

    for copy in slot_copies:
        copy.wait_recv()
    for u in order:
        for x_ in range(XS):
            for j in range(2):
                source = ids_ref[(x_ * mine + u) * 2 + j] // 8
                side = ((source // (2 * ZS) + h) % 2) * 2 + source % 2
                sorted_[x_, u, j] = slots[side, (source // 2) % ZS]
        for d in (2, 1, 3):
            to_handlers[(u, d)] = handler_copy(u, d)
        features[u, :, t] = sorted_[x, u]
        if u in order[:FIRST]:
            across[(u, 0)] = across_copy(u, 0)

    def forward(u):
        if u not in order[:FIRST]:
            across[(u, 0)] = across_copy(u, 0)
        for d in (3, 1, 2):
            to_handlers[(u, d)].wait_recv()
            across[(u, d)] = across_copy(u, (XS - d) % XS)

    for u in order[:AHEAD]:
        forward(u)

    for i in range(XS):
        side_work["q"][i].wait() if i == 0 else side_work["q"][i].wait_recv()
    for copy in side_work["core"]:
        copy.wait_recv()

    def result_rows(span):
        return pl.ds(pl.multiple_of((span + 1) * SPAN, SPAN), SPAN)

    def back(u, d):
        return pltpu.make_async_remote_copy(
            src_ref=results.at[u, d],
            dst_ref=blended.at[result_rows(x * mine + u)],
            send_sem=back_send.at[u, d - 1],
            recv_sem=back_recv.at[u, d - 1],
            device_id=at_tp(x_of[d], l),
            device_id_type=MESH,
        )

    def features_of(u, j):
        source = ids_ref[(x * mine + u) * 2 + j] // 8
        other = (source // (2 * ZS) + h) % 2 == 1
        parts = []
        for k in range(XS):
            low, high = features[u, j, 2 * k], features[u, j, 2 * k + 1]
            parts += [jnp.where(other, high, low), jnp.where(other, low, high)]
        return jnp.concatenate(parts, axis=0)

    for i, u in enumerate(order):
        for d in range(XS):
            across[(u, d)].wait_recv()
        pair = jnp.concatenate([features_of(u, 0), features_of(u, 1)], axis=1)
        for group in GROUPS:
            projected = {
                d: jnp.dot(weights[x_of[d]], pair, preferred_element_type=jnp.float32).astype(
                    jnp.bfloat16
                )
                for d in group
            }
            for d in group:
                wanted = queries[x_of[d], pl.ds(u * SPAN, SPAN + 16)].astype(jnp.float32)
                wanted = wanted[15 : 15 + SPAN].astype(jnp.bfloat16)
                value = heads_of_span(projected[d], wanted, head_count)
                if d == 0:
                    blended[result_rows(x * mine + u)] = value
                else:
                    results[u, d] = value
            for d in group:
                if d > 0:
                    back(u, d).start()
        if i + AHEAD < mine:
            forward(order[i + AHEAD])
        if i == 1:
            for d in range(1, XS):
                back(order[0], d).wait_recv()
            carried = send(blended.at[pl.ds(tokens, SPAN)], blended.at[pl.ds(0, SPAN)], after)

    def shift_out(i):
        rows = blended[pl.ds(i * SPAN, SPAN + 16)].astype(jnp.float32)[1 : 1 + SPAN]
        if i == 0:
            places = lax.broadcasted_iota(jnp.int32, rows.shape, 0)
            rows = jnp.where((s == 0) & (places < SPAN - 1), 0.0, rows)
        out_ref[pl.ds(i * SPAN, SPAN)] = rows.astype(jnp.bfloat16)

    last = [i for i in range(spans) if not EARLY_OUT or order[-1] in (i % mine, (i - 1) % mine)]
    for u in order[1:]:
        if u == order[-1]:
            carried.wait_recv()
            for i in range(spans):
                if i not in last:
                    shift_out(i)
        for d in range(1, XS):
            back(u, d).wait_recv()
    for i in last:
        shift_out(i)
    for copy in sent:
        copy.wait_send()
    for u in order:
        for d in range(1, XS):
            back(u, d).wait_send()


def shards(queries, neighbours, key_weight, value_weight, neighbour_ids):
    tok_rows, columns = queries.shape
    span_count = neighbour_ids.shape[0]
    blocks, depth, length = neighbours.shape
    tps = lax.axis_size("tp")
    ids = neighbour_ids.reshape(-1)
    wanted = (ids // blocks)[None, :] == jnp.arange(1024)[:, None]
    table = jnp.sum(jnp.where(wanted, (ids % blocks)[None, :], 0), axis=1).reshape(8, 128)
    bf16 = jnp.bfloat16
    mine = span_count // XS
    scratch = [pltpu.VMEM((blocks, depth, length), bf16) for _ in range(ZS)]
    scratch += [
        pltpu.VMEM((3, ZS, depth, length), bf16),
        pltpu.VMEM((4, ZS, depth, length), bf16),
        pltpu.VMEM((XS, mine, 2, depth, length), bf16),
        pltpu.VMEM((mine, 2, tps, depth, length), bf16),
        pltpu.VMEM((2, depth * tps, columns), bf16),
        pltpu.VMEM((XS, 2 * columns, depth * tps), bf16),
        pltpu.VMEM((tok_rows + SPAN, columns), bf16),
        pltpu.VMEM((XS, mine * SPAN + 16, columns), bf16),
        pltpu.VMEM((mine, XS, SPAN, columns), bf16),
        pltpu.VMEM((tok_rows + SPAN, columns), bf16),
        pltpu.VMEM((3, 8, 128), jnp.int32),
        pltpu.SMEM((4, 8, 128), jnp.int32),
        pltpu.SemaphoreType.DMA((192,)),
        pltpu.SemaphoreType.DMA((192,)),
        pltpu.SemaphoreType.DMA((16,)),
        pltpu.SemaphoreType.DMA((mine, XS - 1)),
        pltpu.SemaphoreType.DMA((mine, XS - 1)),
    ]
    return pl.pallas_call(
        functools.partial(kernel, head_count=columns // HDIM),
        out_shape=jax.ShapeDtypeStruct((tok_rows, columns), bf16),
        in_specs=[
            pl.BlockSpec(memory_space=pltpu.SMEM),
            pl.BlockSpec(memory_space=pltpu.VMEM),
            pl.BlockSpec(memory_space=pltpu.HBM),
            pl.BlockSpec(memory_space=pltpu.HBM),
            pl.BlockSpec(memory_space=pltpu.HBM),
            pl.BlockSpec(memory_space=pltpu.HBM),
        ],
        out_specs=pl.BlockSpec(memory_space=pltpu.VMEM),
        scratch_shapes=scratch,
        compiler_params=pltpu.CompilerParams(
            collective_id=0, has_side_effects=True, vmem_limit_bytes=63 * 1024 * 1024
        ),
    )(ids, table, neighbours, key_weight, value_weight, queries)


def solution(mesh):
    in_specs = (P("seq", "tp"), P("seq", "tp", None), P(None, "tp"), P(None, "tp"), P("seq", None))
    out_specs = P("seq", "tp")
    return jax.shard_map(shards, mesh=mesh, in_specs=in_specs, out_specs=out_specs, check_vma=False)
```
